512 devices in a mesh: seq: 128 (over y, z, core), section: 4 (over x).
Axes of the slice: x: 4, y: 8, z: 8, core: 2. Of those that a mesh axis runs over, the one named last changes fastest.
Arguments:
- block_input: bfloat16 [4, 32768, 512], P('section', 'seq'), may hold values from -8 to 8
- upstream: bfloat16 [4, 32768, 512], P('section', 'seq'), may hold values from -6 to 6
- w_qkv: bfloat16 [4, 512, 768], P('section'), may hold values from -2 to 2
- w_out: bfloat16 [4, 256, 512], P('section'), may hold values from -0.375 to 0.375
- layer_norm_gain: float32 [4, 512], P('section'), may hold values from 0.1 to 1.9
- layer_norm_bias: float32 [4, 512], P('section'), may hold values from -3 to 3
- send_order: int32 [4, 128, 256], P('section', 'seq'), may hold values from 0 to 255, each once within a row
- recv_order: int32 [4, 128, 256], P('section', 'seq'), may hold values from 0 to 255, each once within a row
- patch_lengths: int32 [4, 128, 2], P('section', 'seq'), may hold values from 1 to 224, 256 in all within a row
Outputs:
- handed: bfloat16 [4, 32768, 512], P('section', 'seq')
The draws below stay inside these ranges and needn't reach their ends.
Inputs may be any that keep to these rules, and one draw needn't show every extreme that they name: `send_order`: each device's row is a permutation of 0 to 255. `recv_order`: each device's row is a permutation of 0 to 255. `patch_lengths`: each device's lengths sum to 256; the largest is at most 224.
All inputs are finite; a program needn't handle non-finite values.
Results may differ from the reference program's by a relative error of at most 0.009.
The reference program's roundings to bfloat16 on the way count: a program that leaves them out, or rounds other values in their place, can miss the bound.
Values may be sent and summed in bfloat16 or wider, within the bound.
No kernel may reach another device: no remote copies, remote signals or barrier semaphores. Data moves between devices by JAX's collectives and lax.ppermute only.
A program may use at most 64 MiB of HBM per device.

```python
import math
import jax
import jax.numpy as jnp
import numpy as np
from jax import lax

D = 512
HEAD = 16
HEADS = 16
ROWS = 256
PATCHES = 2
HD = 256
BLOCK = 2
PATCH_MOST = 224
TOKENS = 32768
SECTIONS = 4
N_SEQ = 128


def draw_block_input(key, part):
    key = jax.random.fold_in(key, 3)
    noise = jax.random.normal(key, (SECTIONS, TOKENS, D), jnp.float32)
    values = noise
    return jnp.clip(values, -8.0, 8.0).astype(jnp.bfloat16)


def draw_w_qkv(key, part):
    key = jax.random.fold_in(key, 4)
    base = jax.random.normal(key, (SECTIONS, D, 3 * HEADS * HEAD), jnp.float32) / math.sqrt(D)
    return jnp.clip(base, -2.0, 2.0).astype(jnp.bfloat16)


def block_levels(stream_key, extent, shards, low, top_value):
    level, own = 1.0, jax.random.fold_in(stream_key, 6)
    for axis_at, blocks in shards:
        steps = jnp.exp(jax.random.uniform(jax.random.fold_in(own, axis_at), (blocks,), jnp.float32, low / len(shards), top_value / len(shards)))
        level = level * jnp.repeat(steps, extent[axis_at] // blocks).reshape([-1 if axis == axis_at else 1 for axis in range(len(extent))])
    return level


def length_profile(count, total, most, slope):
    portions = [(1 << 20) // math.isqrt(grade ** slope) + 1 for grade in range(2, count + 1)]
    rest, counts = total - most - (count - 1), [1] * (count - 1)
    while rest > 0:
        free = [i for i in range(count - 1) if counts[i] < most]
        whole, left = sum([portions[i] for i in free]), rest
        for i in free:
            addition = min(most - counts[i], max(1, left * portions[i] // whole), rest)
            counts[i] = counts[i] + addition
            rest = rest - addition
    return np.array([most] + counts)


def uneven(rng, count, total, reach, lean):
    if count == 2:
        one = jax.random.randint(rng, (), max(1, total - reach), min(reach, total - 1) + 1)
        return jnp.stack([one, total - one])
    sizes = jnp.asarray(length_profile(count, total, reach, lean), jnp.int32)
    couples = (count - 1) // 2
    giver, receiver = sizes[1:1 + 2 * couples:2], sizes[2:2 + 2 * couples:2]
    slack = jnp.minimum(giver - 1, reach - receiver)
    passed = jax.random.randint(jax.random.fold_in(rng, 1), (couples,), 0, 1 << 20) % (slack + 1)
    sizes = sizes.at[1:1 + 2 * couples:2].set(giver - passed).at[2:2 + 2 * couples:2].set(receiver + passed)
    return sizes[jax.random.permutation(jax.random.fold_in(rng, 2), count)]


def scatter_about(stream_key, extent, deviation, reach, shards=(), kind=jnp.bfloat16):
    values = jax.random.normal(stream_key, extent, jnp.float32) * deviation
    if len(shards) > 0:
        values = block_levels(stream_key, extent, shards, -0.22, 0.18) * values
    return jnp.clip(values, min=-reach, max=reach).astype(kind)


def setup_inputs(seed: int = 0) -> dict:
    seeds = jax.random.split(jax.random.key(seed), 10)
    block_input = draw_block_input(jax.random.fold_in(seeds[9], 71), 0)
    upstream = scatter_about(seeds[1], (SECTIONS, TOKENS, D), 1.0, 6.0, ((0, 4), (1, 128)))
    w_qkv = draw_w_qkv(jax.random.fold_in(seeds[9], 71), 0)
    w_out = scatter_about(seeds[3], (SECTIONS, HD, D), HD ** -0.5, 0.375, ((0, 4),))
    layer_norm_gain = jnp.clip(1.0 + 0.18 * jax.random.normal(seeds[4], (SECTIONS, D), jnp.float32), 0.1, 1.9)
    layer_norm_bias = scatter_about(seeds[5], (SECTIONS, D), 0.5, 3.0, ((0, 4),), jnp.float32)
    send_order = jax.vmap(lambda own: jax.random.permutation(own, ROWS))(jax.random.split(seeds[6], SECTIONS * N_SEQ)).reshape((SECTIONS, N_SEQ, ROWS)).astype(jnp.int32)
    recv_order = jax.vmap(lambda own: jax.random.permutation(own, ROWS))(jax.random.split(seeds[7], SECTIONS * N_SEQ)).reshape((SECTIONS, N_SEQ, ROWS)).astype(jnp.int32)
    patch_lengths = jax.vmap(lambda own: uneven(own, PATCHES, ROWS, PATCH_MOST, 2))(jax.random.split(seeds[8], SECTIONS * N_SEQ)).reshape((SECTIONS, N_SEQ, PATCHES)).astype(jnp.int32)
    return dict(block_input=block_input, upstream=upstream, w_qkv=w_qkv, w_out=w_out, layer_norm_gain=layer_norm_gain, layer_norm_bias=layer_norm_bias, send_order=send_order, recv_order=recv_order, patch_lengths=patch_lengths)


def layer_normalize(rows, gain_weight, shift_bias):
    values = rows.astype(jnp.float32)
    centered_rows = values - lax.optimization_barrier(jnp.mean(values, axis=-1, keepdims=True))
    inverse_deviation = lax.rsqrt(lax.optimization_barrier(jnp.mean(centered_rows * centered_rows, axis=-1, keepdims=True)) + 1e-05)
    standardized_input = centered_rows * inverse_deviation
    normalized_rows = (standardized_input * gain_weight + shift_bias).astype(jnp.bfloat16)
    return (normalized_rows, standardized_input, inverse_deviation)

def layer_norm_backward(normed_gradient, standardized_input, inverse_deviation, gain_weight):
    incoming_gradient = normed_gradient * gain_weight
    gradient_mean = lax.optimization_barrier(jnp.mean(incoming_gradient, axis=-1, keepdims=True))
    cross_term_mean = lax.optimization_barrier(jnp.mean(incoming_gradient * standardized_input, axis=-1, keepdims=True))
    return inverse_deviation * (incoming_gradient - gradient_mean - standardized_input * cross_term_mean)

def attend_grad(qkv, out_grad, lengths):
    count = qkv.shape[0]
    width = out_grad.shape[1]
    heads = width // HEAD
    scale = float(HEAD) ** (-0.5)
    bounds = jnp.cumsum(lengths)
    places = jnp.arange(count, dtype=jnp.int32)
    segment = lax.optimization_barrier(jnp.sum((places[:, None] >= bounds[None, :]).astype(jnp.int32), axis=1))
    same = segment[:, None] == segment[None, :]
    contract_last = (((1,), (1,)), ((), ()))
    contract_first = (((0,), (0,)), ((), ()))

    def one_head(head, grads):
        query = lax.dynamic_slice_in_dim(qkv, head * HEAD, HEAD, 1)
        key_part = lax.dynamic_slice_in_dim(qkv, width + head * HEAD, HEAD, 1)
        value = lax.dynamic_slice_in_dim(qkv, 2 * width + head * HEAD, HEAD, 1)
        dout = lax.dynamic_slice_in_dim(out_grad, head * HEAD, HEAD, 1)
        scores = lax.dot_general(query, key_part, contract_last, preferred_element_type=jnp.float32) * scale
        scores = jnp.where(same, scores, -1e+30)
        top = lax.optimization_barrier(jnp.max(scores, axis=-1, keepdims=True))
        expo = jnp.exp(scores - top)
        probs = expo / lax.optimization_barrier(jnp.sum(expo, axis=-1, keepdims=True))
        weights = probs.astype(jnp.bfloat16)
        dprob = lax.dot_general(dout, value, contract_last, preferred_element_type=jnp.float32)
        inner = lax.optimization_barrier(jnp.sum(dprob * probs, axis=-1, keepdims=True))
        dscore = (scale * probs * (dprob - inner)).astype(jnp.bfloat16)
        dquery = jnp.dot(dscore, key_part, preferred_element_type=jnp.float32).astype(jnp.bfloat16)
        dkey = lax.dot_general(dscore, query, contract_first, preferred_element_type=jnp.float32).astype(jnp.bfloat16)
        dvalue = lax.dot_general(weights, dout, contract_first, preferred_element_type=jnp.float32).astype(jnp.bfloat16)
        grads = lax.dynamic_update_slice_in_dim(grads, dquery, head * HEAD, 1)
        grads = lax.dynamic_update_slice_in_dim(grads, dkey, width + head * HEAD, 1)
        grads = lax.dynamic_update_slice_in_dim(grads, dvalue, 2 * width + head * HEAD, 1)
        return grads
    empty = jnp.zeros((count, 3 * width), jnp.bfloat16)
    return lax.fori_loop(0, heads, one_head, empty)

def reference(block_input, upstream, w_qkv, w_out, layer_norm_gain, layer_norm_bias, send_order, recv_order, patch_lengths):
    totals = []
    contract_last = (((1,), (1,)), ((), ()))
    for section_index in range(1, SECTIONS):
        places = recv_order[section_index]
        source_dev = places // BLOCK
        slot = places % BLOCK
        target = jnp.arange(N_SEQ, dtype=jnp.int32)[:, None]
        position = target * BLOCK + slot
        patch_source = (source_dev * ROWS + send_order[section_index][source_dev, position]).reshape(-1).astype(jnp.int32)
        patch_token_rows = block_input[section_index][patch_source]
        normalized_rows, standardized_input, inverse_deviation = layer_normalize(patch_token_rows, layer_norm_gain[section_index], layer_norm_bias[section_index])
        qkv = jnp.dot(normalized_rows, w_qkv[section_index], preferred_element_type=jnp.float32).astype(jnp.bfloat16)
        out_common = lax.dot_general(upstream[section_index], w_out[section_index], contract_last, preferred_element_type=jnp.float32).astype(jnp.bfloat16)
        out_grad = out_common[patch_source]
        dqkv = lax.map(lambda items: attend_grad(items[0], items[1], items[2]), (qkv.reshape(N_SEQ, ROWS, 3 * HD), out_grad.reshape(N_SEQ, ROWS, HD), patch_lengths[section_index]))
        dqkv = dqkv.reshape(TOKENS, 3 * HD)
        normed_gradient = lax.dot_general(dqkv, w_qkv[section_index], contract_last, preferred_element_type=jnp.float32)
        branch_output = layer_norm_backward(normed_gradient, standardized_input, inverse_deviation, layer_norm_gain[section_index]).astype(jnp.bfloat16)
        common = jnp.zeros((TOKENS, D), jnp.bfloat16).at[patch_source].set(branch_output)
        total = (upstream[section_index].astype(jnp.float32) + common.astype(jnp.float32)).astype(jnp.bfloat16)
        totals.append(total)
    handed = jnp.stack(totals + [jnp.zeros((TOKENS, D), jnp.bfloat16)], axis=0)
    return handed
```

```python
import jax
import jax.numpy as jnp
from jax import lax
from jax.experimental import pallas as pl
from jax.experimental.pallas import tpu as pltpu
from jax.sharding import PartitionSpec as P

HEAD = 16
GROUP = 128 // HEAD
MASKED = -(2.0**99)
BF = jnp.bfloat16
F32 = jnp.float32
ROWS_BY_ROWS = (((0,), (0,)), ((), ()))
LAST_BY_LAST = (((1,), (1,)), ((), ()))
ROWS_BY_LAST = (((0,), (1,)), ((), ()))


def dot(a, b, dims=(((1,), (0,)), ((), ()))):
    return lax.dot_general(a, b, dims, preferred_element_type=F32)


def selection(order):
    count = order.shape[1]
    wanted = lax.broadcasted_iota(jnp.int32, (count, count), 0)
    return jnp.where(wanted == order, 1.0, 0.0).astype(BF)


def pre_kernel(rows_ref, upper_ref, w_out_ref, order_ref, sent_ref):
    pick = selection(order_ref[...])
    out_common = dot(upper_ref[0], w_out_ref[0], LAST_BY_LAST).astype(BF)
    both = jnp.concatenate([rows_ref[0], out_common], axis=1)
    sent_ref[...] = dot(pick, both, ROWS_BY_ROWS).astype(BF).reshape(sent_ref.shape)


def main_kernel(got_ref, order_ref, lengths_ref, w_ref, gain_ref, shift_ref, sent_ref, grads_ref):
    count = order_ref.shape[1]
    projection = w_ref[0]
    model = projection.shape[0]
    width = projection.shape[1] // 3
    gain = gain_ref[...]
    place = selection(order_ref[...])
    got = dot(place, got_ref[...].reshape(count, model + width), ROWS_BY_ROWS)

    values = got[:, :model]
    centered = values - jnp.mean(values, axis=-1, keepdims=True)
    inverse = lax.rsqrt(jnp.mean(centered * centered, axis=-1, keepdims=True) + 1e-05)
    standardized = centered * inverse
    normed = (standardized * gain + shift_ref[...]).astype(BF)
    qkv = dot(normed, projection).astype(BF)
    dout = got[:, model:].astype(BF)

    scale = float(HEAD) ** (-0.5)
    query_t = (qkv[:, :width] * scale).T
    key_part = qkv[:, width : 2 * width]
    key_t = (key_part * scale).T
    value = qkv[:, 2 * width :]
    dout_t = dout.T

    first = lengths_ref[0, 0]
    key_at = (lax.broadcasted_iota(jnp.int32, (count, 128), 0) < first).astype(jnp.int32)
    lane = lax.broadcasted_iota(jnp.int32, (count, 128), 1)
    key_mark = jnp.where(lane == key_at, 1.0, 0.0).astype(BF)
    query_at = (lax.broadcasted_iota(jnp.int32, (128, count), 1) >= first).astype(jnp.int32)
    sub = lax.broadcasted_iota(jnp.int32, (128, count), 0)
    query_mark = jnp.where(sub == query_at, MASKED, 0.0).astype(BF)

    for head in range(width // HEAD):
        group, at = divmod(head, GROUP)
        lanes = slice(group * 128, group * 128 + 128)
        mine = slice(head * HEAD, head * HEAD + HEAD)

        def padded(block):
            parts = [block]
            if at > 0:
                parts.insert(0, jnp.zeros((at * HEAD, count), BF))
            if at < GROUP - 1:
                parts.append(jnp.zeros(((GROUP - 1 - at) * HEAD, count), BF))
            return jnp.concatenate(parts, axis=0)

        scores = dot(
            jnp.concatenate([key_part[:, lanes], key_mark], axis=1),
            jnp.concatenate([padded(query_t[mine]), query_mark], axis=0),
        )
        top = jnp.max(scores, axis=0, keepdims=True)
        expo = jnp.exp(scores - top)
        probs = expo * (1.0 / jnp.sum(expo, axis=0, keepdims=True))
        dprob = dot(value[:, lanes], padded(dout_t[mine]))
        inner = jnp.sum(dprob * probs, axis=0, keepdims=True)
        dscore = (probs * (dprob - inner)).astype(BF)
        grads_ref[mine] = dot(key_t[mine], dscore).astype(BF)
        grads_ref[slice(width + mine.start, width + mine.stop)] = dot(
            query_t[mine], dscore, LAST_BY_LAST
        ).astype(BF)
        grads_ref[slice(2 * width + mine.start, 2 * width + mine.stop)] = dot(
            dout_t[mine], probs.astype(BF), LAST_BY_LAST
        ).astype(BF)

    incoming = dot(grads_ref[...], projection, ROWS_BY_LAST) * gain
    mean = jnp.mean(incoming, axis=-1, keepdims=True)
    cross = jnp.mean(incoming * standardized, axis=-1, keepdims=True)
    branch = (inverse * (incoming - mean - standardized * cross)).astype(BF)
    sent_ref[...] = dot(place, branch).astype(BF).reshape(sent_ref.shape)


def post_kernel(got_ref, upper_ref, order_ref, total_ref):
    count, model = total_ref.shape
    branch = dot(selection(order_ref[...]), got_ref[...].reshape(count, model))
    total_ref[...] = (upper_ref[0].astype(F32) + branch).astype(BF)


def regroup(array):
    return lax.all_to_all(array, "seq", split_axis=0, concat_axis=0, tiled=True)


def per_device(
    block_input,
    upstream,
    w_qkv,
    w_out,
    layer_norm_gain,
    layer_norm_bias,
    send_order,
    recv_order,
    patch_lengths,
):
    _, count, model = block_input.shape
    width = w_out.shape[1]
    peers = lax.axis_size("seq")
    each = count // peers
    sending, placing, lengths = send_order[0], recv_order[0], patch_lengths[0]

    sent = pl.pallas_call(
        pre_kernel,
        out_shape=jax.ShapeDtypeStruct((peers, each, model + width), BF),
    )(block_input, upstream, w_out, sending)
    got = regroup(sent)
    vmem = pl.BlockSpec(memory_space=pltpu.VMEM)
    back = pl.pallas_call(
        main_kernel,
        out_shape=jax.ShapeDtypeStruct((peers, each, model), BF),
        in_specs=[vmem, vmem, pl.BlockSpec(memory_space=pltpu.SMEM), vmem, vmem, vmem],
        out_specs=vmem,
        scratch_shapes=[pltpu.VMEM((3 * width, count), BF)],
        compiler_params=pltpu.CompilerParams(vmem_limit_bytes=32 * 1024 * 1024),
    )(got, placing, lengths, w_qkv, layer_norm_gain, layer_norm_bias)
    back = regroup(back)
    total = pl.pallas_call(
        post_kernel,
        out_shape=jax.ShapeDtypeStruct((count, model), BF),
    )(back, upstream, sending)
    sections = lax.axis_size("section")
    handed = lax.ppermute(total, "section", [(s, s - 1) for s in range(1, sections)])
    return handed[None]


def solution(mesh):
    return jax.shard_map(
        per_device,
        mesh=mesh,
        in_specs=(
            P("section", "seq", None),
            P("section", "seq", None),
            P("section", None, None),
            P("section", None, None),
            P("section", None),
            P("section", None),
            P("section", "seq", None),
            P("section", "seq", None),
            P("section", "seq", None),
        ),
        out_specs=P("section", "seq", None),
        check_vma=False,
    )
```

```python
import jax
import jax.numpy as jnp
from jax import lax
from jax.experimental import pallas as pl
from jax.experimental.pallas import tpu as pltpu
from jax.sharding import PartitionSpec as P

HEAD = 16
GROUP = 128 // HEAD
MASKED = -(2.0**99)
BF = jnp.bfloat16
F32 = jnp.float32
ROWS_BY_ROWS = (((0,), (0,)), ((), ()))
LAST_BY_LAST = (((1,), (1,)), ((), ()))
ROWS_BY_LAST = (((0,), (1,)), ((), ()))


def dot(a, b, dims=(((1,), (0,)), ((), ()))):
    return lax.dot_general(a, b, dims, preferred_element_type=F32)


def selection(order):
    count = order.shape[1]
    wanted = lax.broadcasted_iota(jnp.int32, (count, count), 0)
    return jnp.where(wanted == order, 1.0, 0.0).astype(BF)


def pre_kernel(
    rows_hbm, upper_hbm, w_out_hbm, order_hbm, sent_ref, rows_ref, upper_ref, w_out_ref, order_ref, arrived
):
    pairs = [
        (order_hbm, order_ref),
        (upper_hbm.at[0], upper_ref),
        (w_out_hbm.at[0], w_out_ref),
        (rows_hbm.at[0], rows_ref),
    ]
    copies = [pltpu.make_async_copy(a, b, arrived.at[i]) for i, (a, b) in enumerate(pairs)]
    for copy in copies:
        copy.start()
    copies[0].wait()
    pick = selection(order_ref[...])
    copies[1].wait()
    copies[2].wait()
    out_common = dot(upper_ref[...], w_out_ref[...], LAST_BY_LAST).astype(BF)
    copies[3].wait()
    both = jnp.concatenate([rows_ref[...], out_common], axis=1)
    sent_ref[...] = dot(pick, both, ROWS_BY_ROWS).astype(BF).reshape(sent_ref.shape)


def prepare_kernel(
    upper_in,
    sending_in,
    placing_in,
    lengths_in,
    gain_in,
    shift_in,
    upper_ref,
    pick_ref,
    place_ref,
    key_mark_ref,
    query_mark_ref,
    gain_ref,
    shift_ref,
):
    upper_ref[...] = upper_in[0]
    pick_ref[...] = selection(sending_in[...])
    place_ref[...] = selection(placing_in[...])
    gain_ref[...] = gain_in[...]
    shift_ref[...] = shift_in[...]
    first = lengths_in[:, :1]
    count = placing_in.shape[1]
    key_at = (lax.broadcasted_iota(jnp.int32, (count, 128), 0) < first).astype(jnp.int32)
    lane = lax.broadcasted_iota(jnp.int32, (count, 128), 1)
    key_mark_ref[...] = jnp.where(lane == key_at, 1.0, 0.0).astype(BF)
    query_at = (lax.broadcasted_iota(jnp.int32, (128, count), 1) >= first).astype(jnp.int32)
    sub = lax.broadcasted_iota(jnp.int32, (128, count), 0)
    query_mark_ref[...] = jnp.where(sub == query_at, MASKED, 0.0).astype(BF)


def main_kernel(
    got_ref,
    place_ref,
    key_mark_ref,
    query_mark_ref,
    w_ref,
    gain_ref,
    shift_ref,
    sent_ref,
    dscore_ref,
    weights_ref,
    query_ref,
    dout_ref,
    dquery_ref,
    dothers_ref,
):
    count = place_ref.shape[0]
    projection = w_ref[0]
    model = projection.shape[0]
    width = projection.shape[1] // 3
    gain = gain_ref[...]
    place = place_ref[...]
    got = dot(place, got_ref[...].reshape(count, model + width), ROWS_BY_ROWS)

    values = got[:, :model]
    centered = values - jnp.mean(values, axis=-1, keepdims=True)
    inverse = lax.rsqrt(jnp.mean(centered * centered, axis=-1, keepdims=True) + 1e-05)
    standardized = centered * inverse
    normed = (standardized * gain + shift_ref[...]).astype(BF)
    qkv = dot(normed, projection).astype(BF)
    dout = got[:, model:].astype(BF)

    scale = float(HEAD) ** (-0.5)
    query = qkv[:, :width] * scale
    key_part = qkv[:, width : 2 * width]
    value = qkv[:, 2 * width :]
    query_t = query.T
    key_t = (key_part * scale).T
    dout_t = dout.T

    key_mark = key_mark_ref[...]
    query_mark = query_mark_ref[...]
    head_of = lax.broadcasted_iota(jnp.int32, (count, 128), 1) // HEAD

    for head in range(width // HEAD):
        group, at = divmod(head, GROUP)
        lanes = slice(group * 128, group * 128 + 128)
        mine = slice(head * HEAD, head * HEAD + HEAD)
        slot = slice(at * count, at * count + count)

        def padded(block):
            parts = [block]
            if at > 0:
                parts.insert(0, jnp.zeros((at * HEAD, count), BF))
            if at < GROUP - 1:
                parts.append(jnp.zeros(((GROUP - 1 - at) * HEAD, count), BF))
            return jnp.concatenate(parts, axis=0)

        scores = dot(
            jnp.concatenate([key_part[:, lanes], key_mark], axis=1),
            jnp.concatenate([padded(query_t[mine]), query_mark], axis=0),
        )
        dprob = dot(value[:, lanes], padded(dout_t[mine]))
        top = jnp.max(scores, axis=0, keepdims=True)
        expo = jnp.exp(scores - top)
        over = 1.0 / jnp.sum(expo, axis=0, keepdims=True)
        inner = jnp.sum(expo * dprob, axis=0, keepdims=True) * over
        probs = expo * over
        dscore_ref[:, slot] = (probs * (dprob - inner)).astype(BF)
        weights_ref[:, slot] = probs.astype(BF)
        only = (head_of == at).astype(F32).astype(BF)
        query_ref[slot] = query[:, lanes] * only
        dout_ref[slot] = dout[:, lanes] * only
        if at == GROUP - 1:
            dothers_ref[:, lanes] = dot(dscore_ref[...], query_ref[...]).astype(BF)
            dothers_ref[:, slice(width + lanes.start, width + lanes.stop)] = dot(
                weights_ref[...], dout_ref[...]
            ).astype(BF)
            for other in range(GROUP):
                rows = slice(lanes.start + other * HEAD, lanes.start + other * HEAD + HEAD)
                dquery_ref[rows] = dot(
                    key_t[rows], dscore_ref[:, other * count : other * count + count]
                ).astype(BF)

    dnormed = dot(dquery_ref[...], projection[:, :width], ROWS_BY_LAST) + dot(
        dothers_ref[...], projection[:, width:], LAST_BY_LAST
    )
    incoming = dnormed * gain
    mean = jnp.mean(incoming, axis=-1, keepdims=True)
    cross = jnp.mean(incoming * standardized, axis=-1, keepdims=True)
    branch = (inverse * (incoming - mean - standardized * cross)).astype(BF)
    sent_ref[...] = dot(place, branch).astype(BF).reshape(sent_ref.shape)


def post_kernel(got_ref, upper_ref, pick_ref, total_ref):
    branch = dot(pick_ref[...], got_ref[...].reshape(total_ref.shape))
    total_ref[...] = (upper_ref[...].astype(F32) + branch).astype(BF)


def regroup(array):
    return lax.all_to_all(array, "seq", split_axis=0, concat_axis=0, tiled=True)


def per_device(
    block_input,
    upstream,
    w_qkv,
    w_out,
    layer_norm_gain,
    layer_norm_bias,
    send_order,
    recv_order,
    patch_lengths,
):
    _, count, model = block_input.shape
    width = w_out.shape[1]
    peers = lax.axis_size("seq")
    each = count // peers
    sending, placing, lengths = send_order[0], recv_order[0], patch_lengths[0]

    vmem = pl.BlockSpec(memory_space=pltpu.VMEM)
    sent = pl.pallas_call(
        pre_kernel,
        out_shape=jax.ShapeDtypeStruct((peers, each, model + width), BF),
        in_specs=[pl.BlockSpec(memory_space=pltpu.HBM)] * 4,
        out_specs=vmem,
        scratch_shapes=[
            pltpu.VMEM((count, model), BF),
            pltpu.VMEM((count, model), BF),
            pltpu.VMEM((width, model), BF),
            pltpu.VMEM(sending.shape, jnp.int32),
            pltpu.SemaphoreType.DMA((4,)),
        ],
        compiler_params=pltpu.CompilerParams(vmem_limit_bytes=60 * 1024 * 1024),
    )(block_input, upstream, w_out, sending)
    got = regroup(sent)
    upper, pick, place, key_mark, query_mark, gain, shift = pl.pallas_call(
        prepare_kernel,
        out_shape=[
            jax.ShapeDtypeStruct((count, model), BF),
            jax.ShapeDtypeStruct((count, count), BF),
            jax.ShapeDtypeStruct((count, count), BF),
            jax.ShapeDtypeStruct((count, 128), BF),
            jax.ShapeDtypeStruct((128, count), BF),
            jax.ShapeDtypeStruct(layer_norm_gain.shape, F32),
            jax.ShapeDtypeStruct(layer_norm_bias.shape, F32),
        ],
        in_specs=[vmem] * 6,
        out_specs=[vmem] * 7,
        compiler_params=pltpu.CompilerParams(vmem_limit_bytes=8 * 1024 * 1024),
    )(upstream, sending, placing, lengths, layer_norm_gain, layer_norm_bias)
    back = pl.pallas_call(
        main_kernel,
        out_shape=jax.ShapeDtypeStruct((peers, each, model), BF),
        in_specs=[vmem] * 7,
        out_specs=vmem,
        scratch_shapes=[
            pltpu.VMEM((count, GROUP * count), BF),
            pltpu.VMEM((count, GROUP * count), BF),
            pltpu.VMEM((GROUP * count, 128), BF),
            pltpu.VMEM((GROUP * count, 128), BF),
            pltpu.VMEM((width, count), BF),
            pltpu.VMEM((count, 2 * width), BF),
        ],
        compiler_params=pltpu.CompilerParams(vmem_limit_bytes=24 * 1024 * 1024),
    )(got, place, key_mark, query_mark, w_qkv, gain, shift)
    back = regroup(back)
    total = pl.pallas_call(
        post_kernel,
        out_shape=jax.ShapeDtypeStruct((count, model), BF),
        in_specs=[vmem] * 3,
        out_specs=vmem,
        compiler_params=pltpu.CompilerParams(vmem_limit_bytes=8 * 1024 * 1024),
    )(back, upper, pick)
    sections = lax.axis_size("section")
    handed = lax.ppermute(total, "section", [(s, s - 1) for s in range(1, sections)])
    return handed[None]


def solution(mesh):
    return jax.shard_map(
        per_device,
        mesh=mesh,
        in_specs=(
            P("section", "seq", None),
            P("section", "seq", None),
            P("section", None, None),
            P("section", None, None),
            P("section", None),
            P("section", None),
            P("section", "seq", None),
            P("section", "seq", None),
            P("section", "seq", None),
        ),
        out_specs=P("section", "seq", None),
        check_vma=False,
    )
```

```python
import jax
import jax.numpy as jnp
from jax import lax
from jax.experimental import pallas as pl
from jax.experimental.pallas import tpu as pltpu
from jax.sharding import PartitionSpec as P

HEAD = 16
GROUP = 128 // HEAD
MASKED = -(2.0**99)
BF = jnp.bfloat16
F32 = jnp.float32
ROWS_BY_ROWS = (((0,), (0,)), ((), ()))
LAST_BY_LAST = (((1,), (1,)), ((), ()))
ROWS_BY_LAST = (((0,), (1,)), ((), ()))


def dot(a, b, dims=(((1,), (0,)), ((), ()))):
    return lax.dot_general(a, b, dims, preferred_element_type=F32)


def selection(order):
    count = order.shape[1]
    wanted = lax.broadcasted_iota(jnp.int32, (count, count), 0)
    return jnp.where(wanted == order, 1.0, 0.0).astype(BF)


def head_kernel(lanes_ref):
    owner = lax.broadcasted_iota(jnp.int32, lanes_ref.shape, 1) // HEAD
    mine = lax.broadcasted_iota(jnp.int32, lanes_ref.shape, 0)
    lanes_ref[...] = jnp.where(owner == mine, 1.0, 0.0)


def pre_kernel(
    rows_ref,
    upper_ref,
    w_out_ref,
    sending_ref,
    placing_ref,
    lengths_ref,
    gain_in,
    shift_in,
    _,
    sent_ref,
    pick_ref,
    place_ref,
    key_mark_ref,
    query_mark_ref,
    gain_ref,
    shift_ref,
):
    pick = selection(sending_ref[...])
    pick_ref[...] = pick
    out_common = dot(upper_ref[0], w_out_ref[0], LAST_BY_LAST).astype(BF)
    both = jnp.concatenate([rows_ref[0], out_common], axis=1)
    sent_ref[...] = dot(pick, both, ROWS_BY_ROWS).astype(BF).reshape(sent_ref.shape)

    place_ref[...] = selection(placing_ref[...])
    gain_ref[...] = gain_in[...]
    shift_ref[...] = shift_in[...]
    first = lengths_ref[:, :1]
    count = placing_ref.shape[1]
    key_at = (lax.broadcasted_iota(jnp.int32, (count, 128), 0) < first).astype(jnp.int32)
    lane = lax.broadcasted_iota(jnp.int32, (count, 128), 1)
    key_mark_ref[...] = jnp.where(lane == key_at, 1.0, 0.0).astype(BF)
    query_at = (lax.broadcasted_iota(jnp.int32, (128, count), 1) >= first).astype(jnp.int32)
    sub = lax.broadcasted_iota(jnp.int32, (128, count), 0)
    query_mark_ref[...] = jnp.where(sub == query_at, MASKED, 0.0).astype(BF)


def main_kernel(
    got_ref,
    place_ref,
    key_mark_ref,
    query_mark_ref,
    w_ref,
    gain_ref,
    shift_ref,
    head_lanes_ref,
    sent_ref,
    dscore_ref,
    weights_ref,
    query_ref,
    dout_ref,
    dquery_ref,
    dothers_ref,
):
    count = place_ref.shape[0]
    projection = w_ref[0]
    model = projection.shape[0]
    width = projection.shape[1] // 3
    gain = gain_ref[...]
    place = place_ref[...]
    got = dot(place, got_ref[...].reshape(count, model + width), ROWS_BY_ROWS)

    values = got[:, :model]
    centered = values - jnp.mean(values, axis=-1, keepdims=True)
    inverse = lax.rsqrt(jnp.mean(centered * centered, axis=-1, keepdims=True) + 1e-05)
    standardized = centered * inverse
    normed = (standardized * gain + shift_ref[...]).astype(BF)
    qkv = dot(normed, projection).astype(BF)
    dout = got[:, model:].astype(BF)

    scale = float(HEAD) ** (-0.5)
    query = qkv[:, :width] * scale
    key_part = qkv[:, width : 2 * width]
    value = qkv[:, 2 * width :]
    query_t = query.T
    key_t = (key_part * scale).T
    dout_t = dout.T

    key_mark = key_mark_ref[...]
    query_mark = query_mark_ref[...]

    for head in range(width // HEAD):
        group, at = divmod(head, GROUP)
        lanes = slice(group * 128, group * 128 + 128)
        mine = slice(head * HEAD, head * HEAD + HEAD)
        slot = slice(at * count, at * count + count)

        def padded(block):
            parts = [block]
            if at > 0:
                parts.insert(0, jnp.zeros((at * HEAD, count), BF))
            if at < GROUP - 1:
                parts.append(jnp.zeros(((GROUP - 1 - at) * HEAD, count), BF))
            return jnp.concatenate(parts, axis=0)

        scores = dot(
            jnp.concatenate([key_part[:, lanes], key_mark], axis=1),
            jnp.concatenate([padded(query_t[mine]), query_mark], axis=0),
        )
        dprob = dot(value[:, lanes], padded(dout_t[mine]))
        top = jnp.max(scores, axis=0, keepdims=True)
        expo = jnp.exp(scores - top)
        over = 1.0 / jnp.sum(expo, axis=0, keepdims=True)
        inner = jnp.sum(expo * dprob, axis=0, keepdims=True) * over
        probs = expo * over
        dscore_ref[:, slot] = (probs * (dprob - inner)).astype(BF)
        weights_ref[:, slot] = probs.astype(BF)
        only = head_lanes_ref[at : at + 1].astype(BF)
        query_ref[slot] = query[:, lanes] * only
        dout_ref[slot] = dout[:, lanes] * only
        if at == GROUP - 1:
            dothers_ref[:, lanes] = dot(dscore_ref[...], query_ref[...]).astype(BF)
            dothers_ref[:, slice(width + lanes.start, width + lanes.stop)] = dot(
                weights_ref[...], dout_ref[...]
            ).astype(BF)
            for other in range(GROUP):
                rows = slice(lanes.start + other * HEAD, lanes.start + other * HEAD + HEAD)
                dquery_ref[rows] = dot(
                    key_t[rows], dscore_ref[:, other * count : other * count + count]
                ).astype(BF)

    dnormed = dot(dquery_ref[...], projection[:, :width], ROWS_BY_LAST) + dot(
        dothers_ref[...], projection[:, width:], LAST_BY_LAST
    )
    incoming = dnormed * gain
    mean = jnp.mean(incoming, axis=-1, keepdims=True)
    cross = jnp.mean(incoming * standardized, axis=-1, keepdims=True)
    branch = (inverse * (incoming - mean - standardized * cross)).astype(BF)
    sent_ref[...] = dot(place, branch).astype(BF).reshape(sent_ref.shape)


def post_kernel(got_ref, upper_ref, pick_ref, total_ref):
    branch = dot(pick_ref[...], got_ref[...].reshape(total_ref.shape))
    total_ref[...] = (upper_ref[0].astype(F32) + branch).astype(BF)


def regroup(array):
    return lax.all_to_all(array, "seq", split_axis=0, concat_axis=0, tiled=True)


def per_device(
    block_input,
    upstream,
    w_qkv,
    w_out,
    layer_norm_gain,
    layer_norm_bias,
    send_order,
    recv_order,
    patch_lengths,
):
    _, count, model = block_input.shape
    width = w_out.shape[1]
    peers = lax.axis_size("seq")
    each = count // peers
    sending, placing, lengths = send_order[0], recv_order[0], patch_lengths[0]

    vmem = pl.BlockSpec(memory_space=pltpu.VMEM)
    small = pltpu.CompilerParams(vmem_limit_bytes=8 * 1024 * 1024)
    head_lanes = pl.pallas_call(
        head_kernel,
        out_shape=jax.ShapeDtypeStruct((GROUP, 128), F32),
        out_specs=vmem,
        compiler_params=small,
        cost_estimate=pl.CostEstimate(flops=10**10, transcendentals=0, bytes_accessed=10**7),
    )()
    sent, pick, place, key_mark, query_mark, gain, shift = pl.pallas_call(
        pre_kernel,
        out_shape=[
            jax.ShapeDtypeStruct((peers, each, model + width), BF),
            jax.ShapeDtypeStruct((count, count), BF),
            jax.ShapeDtypeStruct((count, count), BF),
            jax.ShapeDtypeStruct((count, 128), BF),
            jax.ShapeDtypeStruct((128, count), BF),
            jax.ShapeDtypeStruct(layer_norm_gain.shape, F32),
            jax.ShapeDtypeStruct(layer_norm_bias.shape, F32),
        ],
        in_specs=[vmem] * 9,
        out_specs=[vmem] * 7,
        compiler_params=small,
    )(
        block_input,
        upstream,
        w_out,
        sending,
        placing,
        lengths,
        layer_norm_gain,
        layer_norm_bias,
        head_lanes,
    )
    got = regroup(sent)
    back = pl.pallas_call(
        main_kernel,
        out_shape=jax.ShapeDtypeStruct((peers, each, model), BF),
        in_specs=[vmem] * 8,
        out_specs=vmem,
        scratch_shapes=[
            pltpu.VMEM((count, GROUP * count), BF),
            pltpu.VMEM((count, GROUP * count), BF),
            pltpu.VMEM((GROUP * count, 128), BF),
            pltpu.VMEM((GROUP * count, 128), BF),
            pltpu.VMEM((width, count), BF),
            pltpu.VMEM((count, 2 * width), BF),
        ],
        compiler_params=pltpu.CompilerParams(vmem_limit_bytes=24 * 1024 * 1024),
    )(got, place, key_mark, query_mark, w_qkv, gain, shift, head_lanes)
    back = regroup(back)
    total = pl.pallas_call(
        post_kernel,
        out_shape=jax.ShapeDtypeStruct((count, model), BF),
        in_specs=[vmem] * 3,
        out_specs=vmem,
        compiler_params=pltpu.CompilerParams(vmem_limit_bytes=8 * 1024 * 1024),
    )(back, upstream, pick)
    sections = lax.axis_size("section")
    handed = lax.ppermute(total, "section", [(s, s - 1) for s in range(1, sections)])
    return handed[None]


def solution(mesh):
    return jax.shard_map(
        per_device,
        mesh=mesh,
        in_specs=(
            P("section", "seq", None),
            P("section", "seq", None),
            P("section", None, None),
            P("section", None, None),
            P("section", None),
            P("section", None),
            P("section", "seq", None),
            P("section", "seq", None),
            P("section", "seq", None),
        ),
        out_specs=P("section", "seq", None),
        check_vma=False,
    )
```

```python
import jax
import jax.numpy as jnp
from jax import lax
from jax.experimental import pallas as pl
from jax.experimental.pallas import tpu as pltpu
from jax.sharding import PartitionSpec as P

HEAD = 16
MASKED = -(2.0**99)
BF = jnp.bfloat16
F32 = jnp.float32
ROWS_BY_ROWS = (((0,), (0,)), ((), ()))
LAST_BY_LAST = (((1,), (1,)), ((), ()))
ROWS_BY_LAST = (((0,), (1,)), ((), ()))


def dot(a, b, dims=(((1,), (0,)), ((), ()))):
    return lax.dot_general(a, b, dims, preferred_element_type=F32)


def selection(numbers, order):
    return jnp.where(numbers == order, 1.0, 0.0).astype(BF)


def number_kernel(numbers_ref):
    numbers_ref[...] = lax.broadcasted_iota(jnp.int32, numbers_ref.shape, 0)


def pre_kernel(
    rows_ref,
    upper_ref,
    w_out_ref,
    sending_ref,
    placing_ref,
    lengths_ref,
    gain_in,
    shift_in,
    numbers_ref,
    sent_ref,
    pick_ref,
    place_ref,
    key_mark_ref,
    query_mark_ref,
    gain_ref,
    shift_ref,
):
    pick = selection(numbers_ref[...], sending_ref[...])
    pick_ref[...] = pick
    out_common = dot(upper_ref[0], w_out_ref[0], LAST_BY_LAST).astype(BF)
    both = jnp.concatenate([rows_ref[0], out_common], axis=1)
    sent_ref[...] = dot(pick, both, ROWS_BY_ROWS).astype(BF).reshape(sent_ref.shape)

    place_ref[...] = selection(numbers_ref[...], placing_ref[...])
    gain_ref[...] = gain_in[...]
    shift_ref[...] = shift_in[...]
    first = lengths_ref[:, :1]
    count = placing_ref.shape[1]
    key_at = (lax.broadcasted_iota(jnp.int32, (count, HEAD), 0) < first).astype(jnp.int32)
    lane = lax.broadcasted_iota(jnp.int32, (count, HEAD), 1)
    key_mark_ref[...] = jnp.where(lane == key_at, 1.0, 0.0).astype(BF)
    query_at = (lax.broadcasted_iota(jnp.int32, (HEAD, count), 1) >= first).astype(jnp.int32)
    sub = lax.broadcasted_iota(jnp.int32, (HEAD, count), 0)
    query_mark_ref[...] = jnp.where(sub == query_at, MASKED, 0.0).astype(BF)


def main_kernel(
    got_ref,
    place_ref,
    key_mark_ref,
    query_mark_ref,
    w_ref,
    gain_ref,
    shift_ref,
    sent_ref,
    dscore_ref,
    weights_ref,
    grads_ref,
):
    count = place_ref.shape[0]
    projection = w_ref[0]
    model = projection.shape[0]
    width = projection.shape[1] // 3
    gain = gain_ref[...]
    place = place_ref[...]
    got = dot(place, got_ref[...].reshape(count, model + width), ROWS_BY_ROWS)

    values = got[:, :model]
    centered = values - jnp.mean(values, axis=-1, keepdims=True)
    inverse = lax.rsqrt(jnp.mean(centered * centered, axis=-1, keepdims=True) + 1e-05)
    standardized = centered * inverse
    normed = (standardized * gain + shift_ref[...]).astype(BF)
    qkv = dot(normed, projection).astype(BF)
    dout = got[:, model:].astype(BF)

    scale = float(HEAD) ** (-0.5)
    query = qkv[:, :width] * scale
    key_part = qkv[:, width : 2 * width]
    value = qkv[:, 2 * width :]
    query_t = query.T
    key_t = (key_part * scale).T
    dout_t = dout.T

    key_mark = key_mark_ref[...]
    query_mark = query_mark_ref[...]

    for head in range(width // HEAD):
        mine = slice(head * HEAD, head * HEAD + HEAD)
        slot = slice(head * count, head * count + count)
        scores = dot(
            jnp.concatenate([key_part[:, mine], key_mark], axis=1),
            jnp.concatenate([query_t[mine], query_mark], axis=0),
        )
        dprob = dot(value[:, mine], dout_t[mine])
        top = jnp.max(scores, axis=0, keepdims=True)
        expo = jnp.exp(scores - top)
        over = 1.0 / jnp.sum(expo, axis=0, keepdims=True)
        inner = jnp.sum(expo * dprob, axis=0, keepdims=True) * over
        probs = expo * over
        dscore_ref[:, slot] = (probs * (dprob - inner)).astype(BF)
        weights_ref[:, slot] = probs.astype(BF)

    for head in range(width // HEAD):
        query_rows = slice(head * HEAD, head * HEAD + HEAD)
        key_rows = slice(width + query_rows.start, width + query_rows.stop)
        value_rows = slice(width + key_rows.start, width + key_rows.stop)
        slot = slice(head * count, head * count + count)
        dscore = dscore_ref[:, slot]
        grads_ref[query_rows] = dot(key_t[query_rows], dscore).astype(BF)
        grads_ref[key_rows] = dot(query_t[query_rows], dscore, LAST_BY_LAST).astype(BF)
        grads_ref[value_rows] = dot(dout_t[query_rows], weights_ref[:, slot], LAST_BY_LAST).astype(BF)

    dnormed = dot(grads_ref[...], projection, ROWS_BY_LAST)
    incoming = dnormed * gain
    mean = jnp.mean(incoming, axis=-1, keepdims=True)
    cross = jnp.mean(incoming * standardized, axis=-1, keepdims=True)
    branch = (inverse * (incoming - mean - standardized * cross)).astype(BF)
    sent_ref[...] = dot(place, branch).astype(BF).reshape(sent_ref.shape)


def post_kernel(got_ref, upper_ref, pick_ref, total_ref):
    branch = dot(pick_ref[...], got_ref[...].reshape(total_ref.shape))
    total_ref[...] = (upper_ref[0].astype(F32) + branch).astype(BF)


def regroup(array):
    return lax.all_to_all(array, "seq", split_axis=0, concat_axis=0, tiled=True)


def per_device(
    block_input,
    upstream,
    w_qkv,
    w_out,
    layer_norm_gain,
    layer_norm_bias,
    send_order,
    recv_order,
    patch_lengths,
):
    _, count, model = block_input.shape
    width = w_out.shape[1]
    peers = lax.axis_size("seq")
    each = count // peers
    sending, placing, lengths = send_order[0], recv_order[0], patch_lengths[0]

    vmem = pl.BlockSpec(memory_space=pltpu.VMEM)
    small = pltpu.CompilerParams(vmem_limit_bytes=8 * 1024 * 1024)
    numbers = pl.pallas_call(
        number_kernel,
        out_shape=jax.ShapeDtypeStruct((count, count), jnp.int32),
        out_specs=vmem,
        compiler_params=small,
        cost_estimate=pl.CostEstimate(flops=10**10, transcendentals=0, bytes_accessed=10**7),
    )()
    sent, pick, place, key_mark, query_mark, gain, shift = pl.pallas_call(
        pre_kernel,
        out_shape=[
            jax.ShapeDtypeStruct((peers, each, model + width), BF),
            jax.ShapeDtypeStruct((count, count), BF),
            jax.ShapeDtypeStruct((count, count), BF),
            jax.ShapeDtypeStruct((count, HEAD), BF),
            jax.ShapeDtypeStruct((HEAD, count), BF),
            jax.ShapeDtypeStruct(layer_norm_gain.shape, F32),
            jax.ShapeDtypeStruct(layer_norm_bias.shape, F32),
        ],
        in_specs=[vmem] * 9,
        out_specs=[vmem] * 7,
        compiler_params=small,
    )(
        block_input,
        upstream,
        w_out,
        sending,
        placing,
        lengths,
        layer_norm_gain,
        layer_norm_bias,
        numbers,
    )
    got = regroup(sent)
    back = pl.pallas_call(
        main_kernel,
        out_shape=jax.ShapeDtypeStruct((peers, each, model), BF),
        in_specs=[vmem] * 7,
        out_specs=vmem,
        scratch_shapes=[
            pltpu.VMEM((count, width // HEAD * count), BF),
            pltpu.VMEM((count, width // HEAD * count), BF),
            pltpu.VMEM((3 * width, count), BF),
        ],
        compiler_params=pltpu.CompilerParams(vmem_limit_bytes=24 * 1024 * 1024),
    )(got, place, key_mark, query_mark, w_qkv, gain, shift)
    back = regroup(back)
    total = pl.pallas_call(
        post_kernel,
        out_shape=jax.ShapeDtypeStruct((count, model), BF),
        in_specs=[vmem] * 3,
        out_specs=vmem,
        compiler_params=pltpu.CompilerParams(vmem_limit_bytes=8 * 1024 * 1024),
    )(back, upstream, pick)
    sections = lax.axis_size("section")
    handed = lax.ppermute(total, "section", [(s, s - 1) for s in range(1, sections)])
    return handed[None]


def solution(mesh):
    return jax.shard_map(
        per_device,
        mesh=mesh,
        in_specs=(
            P("section", "seq", None),
            P("section", "seq", None),
            P("section", None, None),
            P("section", None, None),
            P("section", None),
            P("section", None),
            P("section", "seq", None),
            P("section", "seq", None),
            P("section", "seq", None),
        ),
        out_specs=P("section", "seq", None),
        check_vma=False,
    )
```

```python
import functools

import jax
import jax.numpy as jnp
from jax import lax
from jax.experimental import pallas as pl
from jax.experimental.pallas import tpu as pltpu
from jax.sharding import PartitionSpec as P

HEAD = 16
FIRST = 72
MASKED = -(2.0**99)
BF = jnp.bfloat16
F32 = jnp.float32
ROWS_BY_ROWS = (((0,), (0,)), ((), ()))
LAST_BY_LAST = (((1,), (1,)), ((), ()))
ROWS_BY_LAST = (((0,), (1,)), ((), ()))


def dot(a, b, dims=(((1,), (0,)), ((), ()))):
    return lax.dot_general(a, b, dims, preferred_element_type=F32)


def rotated(order, by):
    return jnp.concatenate([order[:, by:], order[:, :by]], axis=1) if by else order


def selection(numbers, order):
    return jnp.where(numbers == order, 1.0, 0.0).astype(BF)


def number_kernel(numbers_ref):
    numbers_ref[...] = lax.broadcasted_iota(jnp.int32, numbers_ref.shape, 0)


def pre_kernel(
    by,
    rows_ref,
    upper_ref,
    w_out_ref,
    sending_ref,
    placing_ref,
    lengths_ref,
    gain_in,
    shift_in,
    numbers_ref,
    sent_ref,
    pick_ref,
    place_ref,
    key_mark_ref,
    query_mark_ref,
    gain_ref,
    shift_ref,
):
    numbers = numbers_ref[...]
    count = numbers.shape[0]
    pick = selection(numbers, rotated(sending_ref[...], by))
    pick_ref[...] = pick
    out_common = dot(upper_ref[0], w_out_ref[0], LAST_BY_LAST).astype(BF)
    both = jnp.concatenate([rows_ref[0], out_common], axis=1)
    sent_ref[...] = dot(pick, both, ROWS_BY_ROWS).astype(BF).reshape(sent_ref.shape)

    place_ref[...] = selection((numbers + by) % count, placing_ref[...])
    gain_ref[...] = gain_in[...]
    shift_ref[...] = shift_in[...]
    first = lengths_ref[:, :1]
    key_at = (lax.broadcasted_iota(jnp.int32, (count, HEAD), 0) < first).astype(jnp.int32)
    lane = lax.broadcasted_iota(jnp.int32, (count, HEAD), 1)
    key_mark_ref[...] = jnp.where(lane == key_at, 1.0, 0.0).astype(BF)
    query_at = (lax.broadcasted_iota(jnp.int32, (HEAD, count), 1) >= first).astype(jnp.int32)
    sub = lax.broadcasted_iota(jnp.int32, (HEAD, count), 0)
    query_mark_ref[...] = jnp.where(sub == query_at, MASKED, 0.0).astype(BF)


def main_kernel(
    got_ref,
    place_ref,
    key_mark_ref,
    query_mark_ref,
    w_ref,
    gain_ref,
    shift_ref,
    sent_ref,
    dscore_ref,
    weights_ref,
    grads_ref,
):
    count = place_ref.shape[0]
    projection = w_ref[0]
    model = projection.shape[0]
    width = projection.shape[1] // 3
    gain = gain_ref[...]
    place = place_ref[...]
    got = dot(place, got_ref[...].reshape(count, model + width), ROWS_BY_ROWS)

    values = got[:, :model]
    centered = values - jnp.mean(values, axis=-1, keepdims=True)
    inverse = lax.rsqrt(jnp.mean(centered * centered, axis=-1, keepdims=True) + 1e-05)
    standardized = centered * inverse
    normed = (standardized * gain + shift_ref[...]).astype(BF)
    qkv = dot(normed, projection).astype(BF)
    dout = got[:, model:].astype(BF)

    scale = float(HEAD) ** (-0.5)
    query = qkv[:, :width] * scale
    key_part = qkv[:, width : 2 * width]
    value = qkv[:, 2 * width :]
    query_t = query.T
    key_t = (key_part * scale).T
    dout_t = dout.T

    key_mark = key_mark_ref[...]
    query_mark = query_mark_ref[...]

    for head in range(width // HEAD):
        mine = slice(head * HEAD, head * HEAD + HEAD)
        slot = slice(head * count, head * count + count)
        scores = dot(
            jnp.concatenate([key_part[:, mine], key_mark], axis=1),
            jnp.concatenate([query_t[mine], query_mark], axis=0),
        )
        dprob = dot(value[:, mine], dout_t[mine])
        top = jnp.max(scores, axis=0, keepdims=True)
        expo = jnp.exp(scores - top)
        over = 1.0 / jnp.sum(expo, axis=0, keepdims=True)
        inner = jnp.sum(expo * dprob, axis=0, keepdims=True) * over
        probs = expo * over
        dscore_ref[:, slot] = (probs * (dprob - inner)).astype(BF)
        weights_ref[:, slot] = probs.astype(BF)

    for head in range(width // HEAD):
        query_rows = slice(head * HEAD, head * HEAD + HEAD)
        key_rows = slice(width + query_rows.start, width + query_rows.stop)
        value_rows = slice(width + key_rows.start, width + key_rows.stop)
        slot = slice(head * count, head * count + count)
        dscore = dscore_ref[:, slot]
        grads_ref[query_rows] = dot(key_t[query_rows], dscore).astype(BF)
        grads_ref[key_rows] = dot(query_t[query_rows], dscore, LAST_BY_LAST).astype(BF)
        grads_ref[value_rows] = dot(dout_t[query_rows], weights_ref[:, slot], LAST_BY_LAST).astype(BF)

    dnormed = dot(grads_ref[...], projection, ROWS_BY_LAST)
    incoming = dnormed * gain
    mean = jnp.mean(incoming, axis=-1, keepdims=True)
    cross = jnp.mean(incoming * standardized, axis=-1, keepdims=True)
    branch = (inverse * (incoming - mean - standardized * cross)).astype(BF)
    sent_ref[...] = dot(place, branch).astype(BF).reshape(sent_ref.shape)


def post_kernel(got_ref, upper_ref, pick_ref, total_ref):
    branch = dot(pick_ref[...], got_ref[...].reshape(total_ref.shape))
    total_ref[...] = (upper_ref[0].astype(F32) + branch).astype(BF)


def regroup(array):
    peers = array.shape[0]
    ring = [(FIRST + i) % peers for i in range(peers)]
    return lax.all_to_all(
        array, "seq", split_axis=0, concat_axis=0, tiled=True, axis_index_groups=[ring]
    )


def per_device(
    block_input,
    upstream,
    w_qkv,
    w_out,
    layer_norm_gain,
    layer_norm_bias,
    send_order,
    recv_order,
    patch_lengths,
):
    _, count, model = block_input.shape
    width = w_out.shape[1]
    peers = lax.axis_size("seq")
    each = count // peers
    sending, placing, lengths = send_order[0], recv_order[0], patch_lengths[0]

    vmem = pl.BlockSpec(memory_space=pltpu.VMEM)
    small = pltpu.CompilerParams(vmem_limit_bytes=8 * 1024 * 1024)
    numbers = pl.pallas_call(
        number_kernel,
        out_shape=jax.ShapeDtypeStruct((count, count), jnp.int32),
        out_specs=vmem,
        compiler_params=small,
        cost_estimate=pl.CostEstimate(flops=10**10, transcendentals=0, bytes_accessed=10**7),
    )()
    sent, pick, place, key_mark, query_mark, gain, shift = pl.pallas_call(
        functools.partial(pre_kernel, FIRST * each),
        out_shape=[
            jax.ShapeDtypeStruct((peers, each, model + width), BF),
            jax.ShapeDtypeStruct((count, count), BF),
            jax.ShapeDtypeStruct((count, count), BF),
            jax.ShapeDtypeStruct((count, HEAD), BF),
            jax.ShapeDtypeStruct((HEAD, count), BF),
            jax.ShapeDtypeStruct(layer_norm_gain.shape, F32),
            jax.ShapeDtypeStruct(layer_norm_bias.shape, F32),
        ],
        in_specs=[vmem] * 9,
        out_specs=[vmem] * 7,
        compiler_params=small,
    )(
        block_input,
        upstream,
        w_out,
        sending,
        placing,
        lengths,
        layer_norm_gain,
        layer_norm_bias,
        numbers,
    )
    got = regroup(sent)
    back = pl.pallas_call(
        main_kernel,
        out_shape=jax.ShapeDtypeStruct((peers, each, model), BF),
        in_specs=[vmem] * 7,
        out_specs=vmem,
        scratch_shapes=[
            pltpu.VMEM((count, width // HEAD * count), BF),
            pltpu.VMEM((count, width // HEAD * count), BF),
            pltpu.VMEM((3 * width, count), BF),
        ],
        compiler_params=pltpu.CompilerParams(vmem_limit_bytes=24 * 1024 * 1024),
    )(got, place, key_mark, query_mark, w_qkv, gain, shift)
    back = regroup(back)
    total = pl.pallas_call(
        post_kernel,
        out_shape=jax.ShapeDtypeStruct((count, model), BF),
        in_specs=[vmem] * 3,
        out_specs=vmem,
        compiler_params=pltpu.CompilerParams(vmem_limit_bytes=8 * 1024 * 1024),
    )(back, upstream, pick)
    sections = lax.axis_size("section")
    handed = lax.ppermute(total, "section", [(s, s - 1) for s in range(1, sections)])
    return handed[None]


def solution(mesh):
    return jax.shard_map(
        per_device,
        mesh=mesh,
        in_specs=(
            P("section", "seq", None),
            P("section", "seq", None),
            P("section", None, None),
            P("section", None, None),
            P("section", None),
            P("section", None),
            P("section", "seq", None),
            P("section", "seq", None),
            P("section", "seq", None),
        ),
        out_specs=P("section", "seq", None),
        check_vma=False,
    )
```

```python
import functools

import jax
import jax.numpy as jnp
from jax import lax
from jax.experimental import pallas as pl
from jax.experimental.pallas import tpu as pltpu
from jax.sharding import PartitionSpec as P

HEAD = 16
FIRST = 73
MASKED = -(2.0**99)
BF = jnp.bfloat16
F32 = jnp.float32
ROWS_BY_ROWS = (((0,), (0,)), ((), ()))
LAST_BY_LAST = (((1,), (1,)), ((), ()))
ROWS_BY_LAST = (((0,), (1,)), ((), ()))


def dot(a, b, dims=(((1,), (0,)), ((), ()))):
    return lax.dot_general(a, b, dims, preferred_element_type=F32)


def rotated(order, by):
    return jnp.concatenate([order[:, by:], order[:, :by]], axis=1) if by else order


def selection(numbers, order):
    return jnp.where(numbers == order, 1.0, 0.0).astype(BF)


def number_kernel(numbers_ref):
    numbers_ref[...] = lax.broadcasted_iota(jnp.int32, numbers_ref.shape, 0)


def pre_kernel(
    by,
    rows_ref,
    upper_ref,
    w_out_ref,
    sending_ref,
    placing_ref,
    lengths_ref,
    gain_in,
    shift_in,
    numbers_ref,
    sent_ref,
    pick_ref,
    place_ref,
    key_mark_ref,
    query_mark_ref,
    gain_ref,
    shift_ref,
):
    numbers = numbers_ref[...]
    count = numbers.shape[0]
    pick = selection(numbers, rotated(sending_ref[...], by))
    pick_ref[...] = pick
    out_common = dot(upper_ref[0], w_out_ref[0], LAST_BY_LAST).astype(BF)
    both = jnp.concatenate([rows_ref[0], out_common], axis=1)
    sent_ref[...] = dot(pick, both, ROWS_BY_ROWS).astype(BF).reshape(sent_ref.shape)

    place_ref[...] = selection((numbers + by) % count, placing_ref[...])
    gain_ref[...] = gain_in[...]
    shift_ref[...] = shift_in[...]
    first = lengths_ref[:, :1]
    key_at = (lax.broadcasted_iota(jnp.int32, (count, HEAD), 0) < first).astype(jnp.int32)
    lane = lax.broadcasted_iota(jnp.int32, (count, HEAD), 1)
    key_mark_ref[...] = jnp.where(lane == key_at, 1.0, 0.0).astype(BF)
    query_at = (lax.broadcasted_iota(jnp.int32, (HEAD, count), 1) >= first).astype(jnp.int32)
    sub = lax.broadcasted_iota(jnp.int32, (HEAD, count), 0)
    query_mark_ref[...] = jnp.where(sub == query_at, MASKED, 0.0).astype(BF)


def main_kernel(
    got_ref,
    place_ref,
    key_mark_ref,
    query_mark_ref,
    w_ref,
    gain_ref,
    shift_ref,
    sent_ref,
    dscore_ref,
    weights_ref,
    grads_ref,
):
    count = place_ref.shape[0]
    projection = w_ref[0]
    model = projection.shape[0]
    width = projection.shape[1] // 3
    gain = gain_ref[...]
    place = place_ref[...]
    got = dot(place, got_ref[...].reshape(count, model + width), ROWS_BY_ROWS)

    values = got[:, :model]
    centered = values - jnp.mean(values, axis=-1, keepdims=True)
    inverse = lax.rsqrt(jnp.mean(centered * centered, axis=-1, keepdims=True) + 1e-05)
    standardized = centered * inverse
    normed = (standardized * gain + shift_ref[...]).astype(BF)
    qkv = dot(normed, projection).astype(BF)
    dout = got[:, model:].astype(BF)

    scale = float(HEAD) ** (-0.5)
    query = qkv[:, :width] * scale
    key_part = qkv[:, width : 2 * width]
    value = qkv[:, 2 * width :]
    query_t = query.T
    key_t = (key_part * scale).T
    dout_t = dout.T

    key_mark = key_mark_ref[...]
    query_mark = query_mark_ref[...]

    for head in range(width // HEAD):
        mine = slice(head * HEAD, head * HEAD + HEAD)
        slot = slice(head * count, head * count + count)
        scores = dot(
            jnp.concatenate([key_part[:, mine], key_mark], axis=1),
            jnp.concatenate([query_t[mine], query_mark], axis=0),
        )
        dprob = dot(value[:, mine], dout_t[mine])
        top = jnp.max(scores, axis=0, keepdims=True)
        expo = jnp.exp(scores - top)
        over = 1.0 / jnp.sum(expo, axis=0, keepdims=True)
        inner = jnp.sum(expo * dprob, axis=0, keepdims=True) * over
        probs = expo * over
        dscore_ref[:, slot] = (probs * (dprob - inner)).astype(BF)
        weights_ref[:, slot] = probs.astype(BF)

    for head in range(width // HEAD):
        query_rows = slice(head * HEAD, head * HEAD + HEAD)
        key_rows = slice(width + query_rows.start, width + query_rows.stop)
        value_rows = slice(width + key_rows.start, width + key_rows.stop)
        slot = slice(head * count, head * count + count)
        dscore = dscore_ref[:, slot]
        grads_ref[query_rows] = dot(key_t[query_rows], dscore).astype(BF)
        grads_ref[key_rows] = dot(query_t[query_rows], dscore, LAST_BY_LAST).astype(BF)
        grads_ref[value_rows] = dot(dout_t[query_rows], weights_ref[:, slot], LAST_BY_LAST).astype(BF)

    dnormed = dot(grads_ref[...], projection, ROWS_BY_LAST)
    incoming = dnormed * gain
    mean = jnp.mean(incoming, axis=-1, keepdims=True)
    cross = jnp.mean(incoming * standardized, axis=-1, keepdims=True)
    branch = (inverse * (incoming - mean - standardized * cross)).astype(BF)
    sent_ref[...] = dot(place, branch).astype(BF).reshape(sent_ref.shape)


def post_kernel(got_ref, upper_ref, pick_ref, total_ref):
    branch = dot(pick_ref[...], got_ref[...].reshape(total_ref.shape))
    total_ref[...] = (upper_ref[0].astype(F32) + branch).astype(BF)


def regroup(array):
    peers = array.shape[0]
    ring = [(FIRST + i) % peers for i in range(peers)]
    return lax.all_to_all(
        array, "seq", split_axis=0, concat_axis=0, tiled=True, axis_index_groups=[ring]
    )


def per_device(
    block_input,
    upstream,
    w_qkv,
    w_out,
    layer_norm_gain,
    layer_norm_bias,
    send_order,
    recv_order,
    patch_lengths,
):
    _, count, model = block_input.shape
    width = w_out.shape[1]
    peers = lax.axis_size("seq")
    each = count // peers
    sending, placing, lengths = send_order[0], recv_order[0], patch_lengths[0]

    vmem = pl.BlockSpec(memory_space=pltpu.VMEM)
    small = pltpu.CompilerParams(vmem_limit_bytes=8 * 1024 * 1024)
    numbers = pl.pallas_call(
        number_kernel,
        out_shape=jax.ShapeDtypeStruct((count, count), jnp.int32),
        out_specs=vmem,
        compiler_params=small,
        cost_estimate=pl.CostEstimate(flops=10**10, transcendentals=0, bytes_accessed=10**7),
    )()
    sent, pick, place, key_mark, query_mark, gain, shift = pl.pallas_call(
        functools.partial(pre_kernel, FIRST * each),
        out_shape=[
            jax.ShapeDtypeStruct((peers, each, model + width), BF),
            jax.ShapeDtypeStruct((count, count), BF),
            jax.ShapeDtypeStruct((count, count), BF),
            jax.ShapeDtypeStruct((count, HEAD), BF),
            jax.ShapeDtypeStruct((HEAD, count), BF),
            jax.ShapeDtypeStruct(layer_norm_gain.shape, F32),
            jax.ShapeDtypeStruct(layer_norm_bias.shape, F32),
        ],
        in_specs=[vmem] * 9,
        out_specs=[vmem] * 7,
        compiler_params=small,
    )(
        block_input,
        upstream,
        w_out,
        sending,
        placing,
        lengths,
        layer_norm_gain,
        layer_norm_bias,
        numbers,
    )
    got = regroup(sent)
    back = pl.pallas_call(
        main_kernel,
        out_shape=jax.ShapeDtypeStruct((peers, each, model), BF),
        in_specs=[vmem] * 7,
        out_specs=vmem,
        scratch_shapes=[
            pltpu.VMEM((count, width // HEAD * count), BF),
            pltpu.VMEM((count, width // HEAD * count), BF),
            pltpu.VMEM((3 * width, count), BF),
        ],
        compiler_params=pltpu.CompilerParams(vmem_limit_bytes=24 * 1024 * 1024),
    )(got, place, key_mark, query_mark, w_qkv, gain, shift)
    back = regroup(back)
    total = pl.pallas_call(
        post_kernel,
        out_shape=jax.ShapeDtypeStruct((count, model), BF),
        in_specs=[vmem] * 3,
        out_specs=vmem,
        compiler_params=pltpu.CompilerParams(vmem_limit_bytes=8 * 1024 * 1024),
    )(back, upstream, pick)
    sections = lax.axis_size("section")
    handed = lax.ppermute(total, "section", [(s, s - 1) for s in range(1, sections)])
    return handed[None]


def solution(mesh):
    return jax.shard_map(
        per_device,
        mesh=mesh,
        in_specs=(
            P("section", "seq", None),
            P("section", "seq", None),
            P("section", None, None),
            P("section", None, None),
            P("section", None),
            P("section", None),
            P("section", "seq", None),
            P("section", "seq", None),
            P("section", "seq", None),
        ),
        out_specs=P("section", "seq", None),
        check_vma=False,
    )
```

```python
import functools

import jax
import jax.numpy as jnp
from jax import lax
from jax.experimental import pallas as pl
from jax.experimental.pallas import tpu as pltpu
from jax.sharding import PartitionSpec as P

HEAD = 16
FIRST = 73
MASKED = -(2.0**99)
BF = jnp.bfloat16
F32 = jnp.float32
ROWS_BY_ROWS = (((0,), (0,)), ((), ()))
LAST_BY_LAST = (((1,), (1,)), ((), ()))
ROWS_BY_LAST = (((0,), (1,)), ((), ()))


def dot(a, b, dims=(((1,), (0,)), ((), ()))):
    return lax.dot_general(a, b, dims, preferred_element_type=F32)


def rotated(order, by):
    return jnp.concatenate([order[:, by:], order[:, :by]], axis=1) if by else order


def selection(numbers, order):
    return jnp.where(numbers == order, 1.0, 0.0).astype(BF)


def number_kernel(numbers_ref):
    numbers_ref[...] = lax.broadcasted_iota(jnp.int32, numbers_ref.shape, 0)


def pre_kernel(
    by,
    rows_ref,
    upper_ref,
    w_out_ref,
    sending_ref,
    placing_ref,
    lengths_ref,
    gain_in,
    shift_in,
    numbers_ref,
    sent_ref,
    pick_ref,
    place_ref,
    place_t_ref,
    key_mark_ref,
    query_mark_ref,
    gain_ref,
    shift_ref,
):
    numbers = numbers_ref[...]
    count = numbers.shape[0]
    pick = selection(numbers, rotated(sending_ref[...], by))
    pick_ref[...] = pick
    peers, each, _ = sent_ref.shape
    model = rows_ref.shape[2]
    width = w_out_ref.shape[1]
    rows = dot(pick, rows_ref[0], ROWS_BY_ROWS).astype(BF)
    sent_ref[:, :, :model] = rows.reshape(peers, each, model)
    out_common = dot(upper_ref[0], w_out_ref[0], LAST_BY_LAST).astype(BF)
    out_sent = dot(pick, out_common, ROWS_BY_ROWS).astype(BF)
    sent_ref[:, :, model:] = out_sent.reshape(peers, each, width)

    place = selection((numbers + by) % count, placing_ref[...])
    place_ref[...] = place
    place_t_ref[...] = place.T
    gain_ref[...] = gain_in[...]
    shift_ref[...] = shift_in[...]
    first = lengths_ref[:, :1]
    key_at = (lax.broadcasted_iota(jnp.int32, (count, HEAD), 0) < first).astype(jnp.int32)
    lane = lax.broadcasted_iota(jnp.int32, (count, HEAD), 1)
    key_mark_ref[...] = jnp.where(lane == key_at, 1.0, 0.0).astype(BF)
    query_at = (lax.broadcasted_iota(jnp.int32, (HEAD, count), 1) >= first).astype(jnp.int32)
    sub = lax.broadcasted_iota(jnp.int32, (HEAD, count), 0)
    query_mark_ref[...] = jnp.where(sub == query_at, MASKED, 0.0).astype(BF)


def main_kernel(
    got_ref,
    place_ref,
    place_t_ref,
    key_mark_ref,
    query_mark_ref,
    w_ref,
    gain_ref,
    shift_ref,
    sent_ref,
    dscore_ref,
    weights_ref,
    grads_ref,
):
    count = place_ref.shape[0]
    projection = w_ref[0]
    model = projection.shape[0]
    width = projection.shape[1] // 3
    gain = gain_ref[...]
    got = dot(place_t_ref[...], got_ref[...].reshape(count, model + width))

    values = got[:, :model]
    centered = values - jnp.mean(values, axis=-1, keepdims=True)
    inverse = lax.rsqrt(jnp.mean(centered * centered, axis=-1, keepdims=True) + 1e-05)
    standardized = centered * inverse
    normed = (standardized * gain + shift_ref[...]).astype(BF)
    qkv = dot(normed, projection).astype(BF)
    dout = got[:, model:].astype(BF)

    scale = float(HEAD) ** (-0.5)
    query = qkv[:, :width] * scale
    key_part = qkv[:, width : 2 * width]
    value = qkv[:, 2 * width :]
    query_t = query.T
    key_t = (key_part * scale).T
    dout_t = dout.T

    key_mark = key_mark_ref[...]
    query_mark = query_mark_ref[...]

    for head in range(width // HEAD):
        mine = slice(head * HEAD, head * HEAD + HEAD)
        slot = slice(head * count, head * count + count)
        scores = dot(
            jnp.concatenate([key_part[:, mine], key_mark], axis=1),
            jnp.concatenate([query_t[mine], query_mark], axis=0),
        )
        dprob = dot(value[:, mine], dout_t[mine])
        top = jnp.max(scores, axis=0, keepdims=True)
        expo = jnp.exp(scores - top)
        over = 1.0 / jnp.sum(expo, axis=0, keepdims=True)
        inner = jnp.sum(expo * dprob, axis=0, keepdims=True) * over
        probs = expo * over
        dscore_ref[:, slot] = (probs * (dprob - inner)).astype(BF)
        weights_ref[:, slot] = probs.astype(BF)

    for head in range(width // HEAD):
        query_rows = slice(head * HEAD, head * HEAD + HEAD)
        key_rows = slice(width + query_rows.start, width + query_rows.stop)
        value_rows = slice(width + key_rows.start, width + key_rows.stop)
        slot = slice(head * count, head * count + count)
        dscore = dscore_ref[:, slot]
        grads_ref[query_rows] = dot(key_t[query_rows], dscore).astype(BF)
        grads_ref[key_rows] = dot(query_t[query_rows], dscore, LAST_BY_LAST).astype(BF)
        grads_ref[value_rows] = dot(dout_t[query_rows], weights_ref[:, slot], LAST_BY_LAST).astype(BF)

    dnormed = dot(grads_ref[...], projection, ROWS_BY_LAST)
    incoming = dnormed * gain
    mean = jnp.mean(incoming, axis=-1, keepdims=True)
    cross = jnp.mean(incoming * standardized, axis=-1, keepdims=True)
    branch = (inverse * (incoming - mean - standardized * cross)).astype(BF)
    sent_ref[...] = dot(place_ref[...], branch).astype(BF).reshape(sent_ref.shape)


def post_kernel(got_ref, upper_ref, pick_ref, total_ref):
    branch = dot(pick_ref[...], got_ref[...].reshape(total_ref.shape))
    total_ref[...] = (upper_ref[0].astype(F32) + branch).astype(BF)


def regroup(array):
    peers = array.shape[0]
    ring = [(FIRST + i) % peers for i in range(peers)]
    return lax.all_to_all(
        array, "seq", split_axis=0, concat_axis=0, tiled=True, axis_index_groups=[ring]
    )


def per_device(
    block_input,
    upstream,
    w_qkv,
    w_out,
    layer_norm_gain,
    layer_norm_bias,
    send_order,
    recv_order,
    patch_lengths,
):
    _, count, model = block_input.shape
    width = w_out.shape[1]
    peers = lax.axis_size("seq")
    each = count // peers
    sending, placing, lengths = send_order[0], recv_order[0], patch_lengths[0]

    vmem = pl.BlockSpec(memory_space=pltpu.VMEM)
    small = pltpu.CompilerParams(vmem_limit_bytes=8 * 1024 * 1024)
    numbers = pl.pallas_call(
        number_kernel,
        out_shape=jax.ShapeDtypeStruct((count, count), jnp.int32),
        out_specs=vmem,
        compiler_params=small,
        cost_estimate=pl.CostEstimate(flops=10**10, transcendentals=0, bytes_accessed=10**7),
    )()
    sent, pick, place, place_t, key_mark, query_mark, gain, shift = pl.pallas_call(
        functools.partial(pre_kernel, FIRST * each),
        out_shape=[
            jax.ShapeDtypeStruct((peers, each, model + width), BF),
            jax.ShapeDtypeStruct((count, count), BF),
            jax.ShapeDtypeStruct((count, count), BF),
            jax.ShapeDtypeStruct((count, count), BF),
            jax.ShapeDtypeStruct((count, HEAD), BF),
            jax.ShapeDtypeStruct((HEAD, count), BF),
            jax.ShapeDtypeStruct(layer_norm_gain.shape, F32),
            jax.ShapeDtypeStruct(layer_norm_bias.shape, F32),
        ],
        in_specs=[vmem] * 9,
        out_specs=[vmem] * 8,
        compiler_params=small,
    )(
        block_input,
        upstream,
        w_out,
        sending,
        placing,
        lengths,
        layer_norm_gain,
        layer_norm_bias,
        numbers,
    )
    got = regroup(sent)
    back = pl.pallas_call(
        main_kernel,
        out_shape=jax.ShapeDtypeStruct((peers, each, model), BF),
        in_specs=[vmem] * 8,
        out_specs=vmem,
        scratch_shapes=[
            pltpu.VMEM((count, width // HEAD * count), BF),
            pltpu.VMEM((count, width // HEAD * count), BF),
            pltpu.VMEM((3 * width, count), BF),
        ],
        compiler_params=pltpu.CompilerParams(vmem_limit_bytes=24 * 1024 * 1024),
    )(got, place, place_t, key_mark, query_mark, w_qkv, gain, shift)
    back = regroup(back)
    total = pl.pallas_call(
        post_kernel,
        out_shape=jax.ShapeDtypeStruct((count, model), BF),
        in_specs=[vmem] * 3,
        out_specs=vmem,
        compiler_params=pltpu.CompilerParams(vmem_limit_bytes=8 * 1024 * 1024),
    )(back, upstream, pick)
    sections = lax.axis_size("section")
    handed = lax.ppermute(total, "section", [(s, s - 1) for s in range(1, sections)])
    return handed[None]


def solution(mesh):
    return jax.shard_map(
        per_device,
        mesh=mesh,
        in_specs=(
            P("section", "seq", None),
            P("section", "seq", None),
            P("section", None, None),
            P("section", None, None),
            P("section", None),
            P("section", None),
            P("section", "seq", None),
            P("section", "seq", None),
            P("section", "seq", None),
        ),
        out_specs=P("section", "seq", None),
        check_vma=False,
    )
```

```python
import functools

import jax
import jax.numpy as jnp
from jax import lax
from jax.experimental import pallas as pl
from jax.experimental.pallas import tpu as pltpu
from jax.sharding import PartitionSpec as P

HEAD = 16
FIRST = 73
MASKED = -(2.0**99)
BF = jnp.bfloat16
F32 = jnp.float32
ROWS_BY_ROWS = (((0,), (0,)), ((), ()))
LAST_BY_LAST = (((1,), (1,)), ((), ()))
ROWS_BY_LAST = (((0,), (1,)), ((), ()))


def dot(a, b, dims=(((1,), (0,)), ((), ()))):
    return lax.dot_general(a, b, dims, preferred_element_type=F32)


def rotated(order, by):
    return jnp.concatenate([order[:, by:], order[:, :by]], axis=1) if by else order


def selection(numbers, order):
    return jnp.where(numbers == order, 1.0, 0.0).astype(BF)


def number_kernel(numbers_ref):
    numbers_ref[...] = lax.broadcasted_iota(jnp.int32, numbers_ref.shape, 0)


def pre_kernel(
    by,
    rows_ref,
    upper_ref,
    w_out_ref,
    sending_ref,
    placing_ref,
    lengths_ref,
    gain_in,
    shift_in,
    numbers_ref,
    sent_ref,
    pick_ref,
    place_ref,
    place_t_ref,
    key_mark_ref,
    query_mark_ref,
    gain_ref,
    shift_ref,
):
    numbers = numbers_ref[...]
    count = numbers.shape[0]
    pick = selection(numbers, rotated(sending_ref[...], by))
    pick_ref[...] = pick
    out_common = dot(upper_ref[0], w_out_ref[0], LAST_BY_LAST).astype(BF)
    both = jnp.concatenate([rows_ref[0], out_common], axis=1)
    sent_ref[...] = dot(pick, both, ROWS_BY_ROWS).astype(BF).reshape(sent_ref.shape)

    place = selection((numbers + by) % count, placing_ref[...])
    place_ref[...] = place
    place_t_ref[...] = place.T
    gain_ref[...] = gain_in[...]
    shift_ref[...] = shift_in[...]
    first = lengths_ref[:, :1]
    key_at = (lax.broadcasted_iota(jnp.int32, (count, HEAD), 0) < first).astype(jnp.int32)
    lane = lax.broadcasted_iota(jnp.int32, (count, HEAD), 1)
    key_mark_ref[...] = jnp.where(lane == key_at, 1.0, 0.0).astype(BF)
    query_at = (lax.broadcasted_iota(jnp.int32, (HEAD, count), 1) >= first).astype(jnp.int32)
    sub = lax.broadcasted_iota(jnp.int32, (HEAD, count), 0)
    query_mark_ref[...] = jnp.where(sub == query_at, MASKED, 0.0).astype(BF)


def main_kernel(
    got_ref,
    place_ref,
    place_t_ref,
    key_mark_ref,
    query_mark_ref,
    w_ref,
    gain_ref,
    shift_ref,
    sent_ref,
    dscore_ref,
    weights_ref,
    grads_ref,
):
    count = place_ref.shape[0]
    projection = w_ref[0]
    model = projection.shape[0]
    width = projection.shape[1] // 3
    gain = gain_ref[...]
    got = dot(place_t_ref[...], got_ref[...].reshape(count, model + width))

    values = got[:, :model]
    centered = values - jnp.mean(values, axis=-1, keepdims=True)
    inverse = lax.rsqrt(jnp.mean(centered * centered, axis=-1, keepdims=True) + 1e-05)
    standardized = centered * inverse
    normed = (standardized * gain + shift_ref[...]).astype(BF)
    qkv = dot(normed, projection).astype(BF)
    dout = got[:, model:].astype(BF)

    scale = float(HEAD) ** (-0.5)
    query = qkv[:, :width] * scale
    key_part = qkv[:, width : 2 * width]
    value = qkv[:, 2 * width :]
    query_t = query.T
    key_t = (key_part * scale).T
    dout_t = dout.T

    key_mark = key_mark_ref[...]
    query_mark = query_mark_ref[...]

    for head in range(width // HEAD):
        mine = slice(head * HEAD, head * HEAD + HEAD)
        slot = slice(head * count, head * count + count)
        scores = dot(
            jnp.concatenate([key_part[:, mine], key_mark], axis=1),
            jnp.concatenate([query_t[mine], query_mark], axis=0),
        )
        dprob = dot(value[:, mine], dout_t[mine])
        top = jnp.max(scores, axis=0, keepdims=True)
        expo = jnp.exp(scores - top)
        over = 1.0 / jnp.sum(expo, axis=0, keepdims=True)
        inner = jnp.sum(expo * dprob, axis=0, keepdims=True) * over
        probs = expo * over
        dscore_ref[:, slot] = (probs * (dprob - inner)).astype(BF)
        weights_ref[:, slot] = probs.astype(BF)

    for head in range(width // HEAD):
        query_rows = slice(head * HEAD, head * HEAD + HEAD)
        key_rows = slice(width + query_rows.start, width + query_rows.stop)
        value_rows = slice(width + key_rows.start, width + key_rows.stop)
        slot = slice(head * count, head * count + count)
        dscore = dscore_ref[:, slot]
        grads_ref[query_rows] = dot(key_t[query_rows], dscore).astype(BF)
        grads_ref[key_rows] = dot(query_t[query_rows], dscore, LAST_BY_LAST).astype(BF)
        grads_ref[value_rows] = dot(dout_t[query_rows], weights_ref[:, slot], LAST_BY_LAST).astype(BF)

    dnormed = dot(grads_ref[...], projection, ROWS_BY_LAST)
    incoming = dnormed * gain
    mean = jnp.mean(incoming, axis=-1, keepdims=True)
    cross = jnp.mean(incoming * standardized, axis=-1, keepdims=True)
    branch = (inverse * (incoming - mean - standardized * cross)).astype(BF)
    sent_ref[...] = dot(place_ref[...], branch).astype(BF).reshape(sent_ref.shape)


def post_kernel(got_ref, upper_ref, pick_ref, total_ref):
    branch = dot(pick_ref[...], got_ref[...].reshape(total_ref.shape))
    total_ref[...] = (upper_ref[0].astype(F32) + branch).astype(BF)


def regroup(array):
    peers = array.shape[0]
    ring = [(FIRST + i) % peers for i in range(peers)]
    return lax.all_to_all(
        array, "seq", split_axis=0, concat_axis=0, tiled=True, axis_index_groups=[ring]
    )


def per_device(
    block_input,
    upstream,
    w_qkv,
    w_out,
    layer_norm_gain,
    layer_norm_bias,
    send_order,
    recv_order,
    patch_lengths,
):
    _, count, model = block_input.shape
    width = w_out.shape[1]
    peers = lax.axis_size("seq")
    each = count // peers
    sending, placing, lengths = send_order[0], recv_order[0], patch_lengths[0]

    vmem = pl.BlockSpec(memory_space=pltpu.VMEM)
    small = pltpu.CompilerParams(vmem_limit_bytes=8 * 1024 * 1024)
    numbers = pl.pallas_call(
        number_kernel,
        out_shape=jax.ShapeDtypeStruct((count, count), jnp.int32),
        out_specs=vmem,
        compiler_params=small,
        cost_estimate=pl.CostEstimate(flops=10**10, transcendentals=0, bytes_accessed=10**7),
    )()
    sent, pick, place, place_t, key_mark, query_mark, gain, shift = pl.pallas_call(
        functools.partial(pre_kernel, FIRST * each),
        out_shape=[
            jax.ShapeDtypeStruct((peers, each, model + width), BF),
            jax.ShapeDtypeStruct((count, count), BF),
            jax.ShapeDtypeStruct((count, count), BF),
            jax.ShapeDtypeStruct((count, count), BF),
            jax.ShapeDtypeStruct((count, HEAD), BF),
            jax.ShapeDtypeStruct((HEAD, count), BF),
            jax.ShapeDtypeStruct(layer_norm_gain.shape, F32),
            jax.ShapeDtypeStruct(layer_norm_bias.shape, F32),
        ],
        in_specs=[vmem] * 9,
        out_specs=[vmem] * 8,
        compiler_params=small,
    )(
        block_input,
        upstream,
        w_out,
        sending,
        placing,
        lengths,
        layer_norm_gain,
        layer_norm_bias,
        numbers,
    )
    got = regroup(sent)
    back = pl.pallas_call(
        main_kernel,
        out_shape=jax.ShapeDtypeStruct((peers, each, model), BF),
        in_specs=[vmem] * 8,
        out_specs=vmem,
        scratch_shapes=[
            pltpu.VMEM((count, width // HEAD * count), BF),
            pltpu.VMEM((count, width // HEAD * count), BF),
            pltpu.VMEM((3 * width, count), BF),
        ],
        compiler_params=pltpu.CompilerParams(vmem_limit_bytes=24 * 1024 * 1024),
    )(got, place, place_t, key_mark, query_mark, w_qkv, gain, shift)
    back = regroup(back)
    total = pl.pallas_call(
        post_kernel,
        out_shape=jax.ShapeDtypeStruct((count, model), BF),
        in_specs=[vmem] * 3,
        out_specs=vmem,
        compiler_params=pltpu.CompilerParams(vmem_limit_bytes=8 * 1024 * 1024),
    )(back, upstream, pick)
    sections = lax.axis_size("section")
    handed = lax.ppermute(total, "section", [(s, s - 1) for s in range(1, sections)])
    return handed[None]


def solution(mesh):
    return jax.shard_map(
        per_device,
        mesh=mesh,
        in_specs=(
            P("section", "seq", None),
            P("section", "seq", None),
            P("section", None, None),
            P("section", None, None),
            P("section", None),
            P("section", None),
            P("section", "seq", None),
            P("section", "seq", None),
            P("section", "seq", None),
        ),
        out_specs=P("section", "seq", None),
        check_vma=False,
    )
```

```python
import functools

import jax
import jax.numpy as jnp
from jax import lax
from jax.experimental import pallas as pl
from jax.experimental.pallas import tpu as pltpu
from jax.sharding import PartitionSpec as P

HEAD = 16
FIRST = 73
MASKED = -(2.0**99)
BF = jnp.bfloat16
F32 = jnp.float32
ROWS_BY_ROWS = (((0,), (0,)), ((), ()))
LAST_BY_LAST = (((1,), (1,)), ((), ()))
ROWS_BY_LAST = (((0,), (1,)), ((), ()))


def dot(a, b, dims=(((1,), (0,)), ((), ()))):
    return lax.dot_general(a, b, dims, preferred_element_type=F32)


def rotated(order, by):
    return jnp.concatenate([order[:, by:], order[:, :by]], axis=1) if by else order


def selection(numbers, order):
    return jnp.where(numbers == order, 1.0, 0.0).astype(BF)


def number_kernel(numbers_ref):
    numbers_ref[...] = lax.broadcasted_iota(jnp.int32, numbers_ref.shape, 0)


def pre_kernel(
    by,
    rows_ref,
    upper_ref,
    w_out_ref,
    sending_ref,
    placing_ref,
    lengths_ref,
    gain_in,
    shift_in,
    numbers_ref,
    sent_ref,
    pick_ref,
    place_ref,
    place_t_ref,
    key_mark_ref,
    query_mark_ref,
    gain_ref,
    shift_ref,
):
    numbers = numbers_ref[...]
    count = numbers.shape[0]
    pick = selection(numbers, rotated(sending_ref[...], by))
    pick_ref[...] = pick
    out_common = dot(upper_ref[0], w_out_ref[0], LAST_BY_LAST).astype(BF)
    both = jnp.concatenate([rows_ref[0], out_common], axis=1)
    sent_ref[...] = dot(pick, both, ROWS_BY_ROWS).astype(BF).reshape(sent_ref.shape)

    place = selection((numbers + by) % count, placing_ref[...])
    place_ref[...] = place
    place_t_ref[...] = place.T
    gain_ref[...] = gain_in[...]
    shift_ref[...] = shift_in[...]
    first = lengths_ref[:, :1]
    key_at = (lax.broadcasted_iota(jnp.int32, (count, HEAD), 0) < first).astype(jnp.int32)
    lane = lax.broadcasted_iota(jnp.int32, (count, HEAD), 1)
    key_mark_ref[...] = jnp.where(lane == key_at, 1.0, 0.0).astype(BF)
    query_at = (lax.broadcasted_iota(jnp.int32, (HEAD, count), 1) >= first).astype(jnp.int32)
    sub = lax.broadcasted_iota(jnp.int32, (HEAD, count), 0)
    query_mark_ref[...] = jnp.where(sub == query_at, MASKED, 0.0).astype(BF)


def main_kernel(
    got_ref,
    place_ref,
    place_t_ref,
    key_mark_ref,
    query_mark_ref,
    w_ref,
    gain_ref,
    shift_ref,
    sent_ref,
    dscore_ref,
    weights_ref,
    grads_ref,
):
    count = place_ref.shape[0]
    projection = w_ref[0]
    model = projection.shape[0]
    width = projection.shape[1] // 3
    gain = gain_ref[...]
    got = dot(place_t_ref[...], got_ref[...].reshape(count, model + width))

    values = got[:, :model]
    centered = values - jnp.mean(values, axis=-1, keepdims=True)
    inverse = lax.rsqrt(jnp.mean(centered * centered, axis=-1, keepdims=True) + 1e-05)
    standardized = centered * inverse
    normed = (standardized * gain + shift_ref[...]).astype(BF)
    qkv = dot(normed, projection).astype(BF)
    dout = got[:, model:].astype(BF)

    scale = float(HEAD) ** (-0.5)
    query = qkv[:, :width] * scale
    key_part = qkv[:, width : 2 * width]
    value = qkv[:, 2 * width :]
    query_t = query.T
    key_t = (key_part * scale).T
    dout_t = dout.T

    key_mark = key_mark_ref[...]
    query_mark = query_mark_ref[...]

    for head in range(width // HEAD):
        mine = slice(head * HEAD, head * HEAD + HEAD)
        slot = slice(head * count, head * count + count)
        scores = dot(
            jnp.concatenate([key_part[:, mine], key_mark], axis=1),
            jnp.concatenate([query_t[mine], query_mark], axis=0),
        )
        dprob = dot(value[:, mine], dout_t[mine])
        top = jnp.max(scores, axis=0, keepdims=True)
        expo = jnp.exp(scores - top)
        over = 1.0 / jnp.sum(expo, axis=0, keepdims=True)
        inner = jnp.sum(expo * dprob, axis=0, keepdims=True) * over
        probs = expo * over
        dscore_ref[:, slot] = (probs * (dprob - inner)).astype(BF)
        weights_ref[:, slot] = probs.astype(BF)

    for head in range(width // HEAD):
        query_rows = slice(head * HEAD, head * HEAD + HEAD)
        key_rows = slice(width + query_rows.start, width + query_rows.stop)
        value_rows = slice(width + key_rows.start, width + key_rows.stop)
        slot = slice(head * count, head * count + count)
        dscore = dscore_ref[:, slot]
        grads_ref[query_rows] = dot(key_t[query_rows], dscore).astype(BF)
        grads_ref[key_rows] = dot(query_t[query_rows], dscore, LAST_BY_LAST).astype(BF)
        grads_ref[value_rows] = dot(dout_t[query_rows], weights_ref[:, slot], LAST_BY_LAST).astype(BF)

    dnormed = sum(
        dot(grads_ref[at : at + width], projection[:, at : at + width], ROWS_BY_LAST)
        for at in range(0, 3 * width, width)
    )
    incoming = dnormed * gain
    mean = jnp.mean(incoming, axis=-1, keepdims=True)
    cross = jnp.mean(incoming * standardized, axis=-1, keepdims=True)
    branch = (inverse * (incoming - mean - standardized * cross)).astype(BF)
    sent_ref[...] = dot(place_ref[...], branch).astype(BF).reshape(sent_ref.shape)


def post_kernel(got_ref, upper_ref, pick_ref, total_ref):
    branch = dot(pick_ref[...], got_ref[...].reshape(total_ref.shape))
    total_ref[...] = (upper_ref[0].astype(F32) + branch).astype(BF)


def regroup(array):
    peers = array.shape[0]
    ring = [(FIRST + i) % peers for i in range(peers)]
    return lax.all_to_all(
        array, "seq", split_axis=0, concat_axis=0, tiled=True, axis_index_groups=[ring]
    )


def per_device(
    block_input,
    upstream,
    w_qkv,
    w_out,
    layer_norm_gain,
    layer_norm_bias,
    send_order,
    recv_order,
    patch_lengths,
):
    _, count, model = block_input.shape
    width = w_out.shape[1]
    peers = lax.axis_size("seq")
    each = count // peers
    sending, placing, lengths = send_order[0], recv_order[0], patch_lengths[0]

    vmem = pl.BlockSpec(memory_space=pltpu.VMEM)
    small = pltpu.CompilerParams(vmem_limit_bytes=8 * 1024 * 1024)
    numbers = pl.pallas_call(
        number_kernel,
        out_shape=jax.ShapeDtypeStruct((count, count), jnp.int32),
        out_specs=vmem,
        compiler_params=small,
        cost_estimate=pl.CostEstimate(flops=10**10, transcendentals=0, bytes_accessed=10**7),
    )()
    sent, pick, place, place_t, key_mark, query_mark, gain, shift = pl.pallas_call(
        functools.partial(pre_kernel, FIRST * each),
        out_shape=[
            jax.ShapeDtypeStruct((peers, each, model + width), BF),
            jax.ShapeDtypeStruct((count, count), BF),
            jax.ShapeDtypeStruct((count, count), BF),
            jax.ShapeDtypeStruct((count, count), BF),
            jax.ShapeDtypeStruct((count, HEAD), BF),
            jax.ShapeDtypeStruct((HEAD, count), BF),
            jax.ShapeDtypeStruct(layer_norm_gain.shape, F32),
            jax.ShapeDtypeStruct(layer_norm_bias.shape, F32),
        ],
        in_specs=[vmem] * 9,
        out_specs=[vmem] * 8,
        compiler_params=small,
    )(
        block_input,
        upstream,
        w_out,
        sending,
        placing,
        lengths,
        layer_norm_gain,
        layer_norm_bias,
        numbers,
    )
    got = regroup(sent)
    back = pl.pallas_call(
        main_kernel,
        out_shape=jax.ShapeDtypeStruct((peers, each, model), BF),
        in_specs=[vmem] * 8,
        out_specs=vmem,
        scratch_shapes=[
            pltpu.VMEM((count, width // HEAD * count), BF),
            pltpu.VMEM((count, width // HEAD * count), BF),
            pltpu.VMEM((3 * width, count), BF),
        ],
        compiler_params=pltpu.CompilerParams(vmem_limit_bytes=24 * 1024 * 1024),
    )(got, place, place_t, key_mark, query_mark, w_qkv, gain, shift)
    back = regroup(back)
    total = pl.pallas_call(
        post_kernel,
        out_shape=jax.ShapeDtypeStruct((count, model), BF),
        in_specs=[vmem] * 3,
        out_specs=vmem,
        compiler_params=pltpu.CompilerParams(vmem_limit_bytes=8 * 1024 * 1024),
    )(back, upstream, pick)
    sections = lax.axis_size("section")
    handed = lax.ppermute(total, "section", [(s, s - 1) for s in range(1, sections)])
    return handed[None]


def solution(mesh):
    return jax.shard_map(
        per_device,
        mesh=mesh,
        in_specs=(
            P("section", "seq", None),
            P("section", "seq", None),
            P("section", None, None),
            P("section", None, None),
            P("section", None),
            P("section", None),
            P("section", "seq", None),
            P("section", "seq", None),
            P("section", "seq", None),
        ),
        out_specs=P("section", "seq", None),
        check_vma=False,
    )
```
